256 devices in a mesh: row: 32 (over y_hi, z, core), rep: 8 (over y_lo, x).
Axes of the slice: x: 4, y: 4 (y_hi: 2, y_lo: 2; y = y_hi * 2 + y_lo), z: 8, core: 2. Of those that a mesh axis runs over, the one named last changes fastest.
Arguments:
- features: bfloat16 [24576, 256], P('row'), may hold values from -7 to 7
- adjacency: bfloat16 [24576, 24576], P('row', 'rep'), may hold values from -0.078125 to 0.078125
- tile_live: int32 [32, 32], P('row', 'rep'), may hold values from 0 to 1, as said below
- w_self: bfloat16 [256, 256], replicated, may hold values from -1.25 to 1.25
- w_neigh: bfloat16 [256, 256], replicated, may hold values from -1.25 to 1.25
- bias_vector: float32 [256], replicated, may hold values from -3 to 3
- pos_pairs: int32 [32, 1024, 3], P('row', 'rep'), may hold values from 0 to 640, as said below
- neg_pairs: int32 [32, 1024, 3], P('row', 'rep'), may hold values from 0 to 640, as said below
Outputs:
- embedding: bfloat16 [24576, 256], P(('row', 'rep'))
- pos_loss: float32 [32, 1024, 128], P('row', 'rep')
- neg_loss: float32 [32, 1024, 128], P('row', 'rep')
The draws below stay inside these ranges and needn't reach their ends.
Inputs may be any that keep to these rules, and one draw needn't show every extreme that they name: `tile_live`: 1 marks a tile that counts (the adjacency holds nonzero values in every tile, live or not); every diagonal tile is live. `pos_pairs`: column 0 is below 6, column 1 below 4, column 2 at most 640, which is reached. `neg_pairs`: column 0 is below 6, column 1 below 4, column 2 at most 640, which is reached.
All inputs are finite; a program needn't handle non-finite values.
Results may differ from the reference program's by a relative error of at most 0.0037.
Values may be sent and summed in bfloat16 or wider, within the bound.
A program may use at most 128 MiB of HBM per device.

```python
import math
import jax
import jax.numpy as jnp
from jax import lax

F = 256
BLOCK = 768
PAIRS = 128
PAIR_ROWS = 128
NODES = 24576
N_ROW = 32
N_REP = 8


def pair_table(key):
    first = jax.random.randint(jax.random.fold_in(key, 1), (N_ROW, N_REP * PAIRS), 0, BLOCK // PAIR_ROWS)
    second = jax.random.randint(jax.random.fold_in(key, 2), (N_ROW, N_REP * PAIRS), 0, N_ROW // N_REP)
    offsets = jax.random.randint(jax.random.fold_in(key, 3), (N_ROW, N_REP * PAIRS), 0, BLOCK - PAIR_ROWS + 1)
    offsets = offsets.at[0, 0].set(BLOCK - PAIR_ROWS)
    offsets = offsets.at[0, 1].set(0)
    return jnp.stack([first, second, offsets], axis=-1).astype(jnp.int32)


def signed_diagonal(key, noise, spread):
    signs = (jax.random.randint(jax.random.fold_in(key, 1), (F,), 0, 2) * 2 - 1).astype(jnp.float32)
    rows_idx = jnp.arange(F, dtype=jnp.int32)[:, None]
    cols_idx = jnp.arange(F, dtype=jnp.int32)[None, :]
    diagonal = jnp.where(rows_idx == cols_idx, signs[:, None], 0.0)
    return (diagonal + noise * (spread / jnp.sqrt(jnp.float32(F)))).astype(jnp.bfloat16)


def draw_features(key, part):
    key = jax.random.fold_in(key, 5)
    block_keys = jax.random.split(jax.random.fold_in(key, 1), N_ROW)
    ranks = jax.vmap(lambda one_key: jax.random.permutation(one_key, F))(block_keys)
    spread = jnp.exp(jnp.log(3.0) * (ranks.astype(jnp.float32) / (F - 1) - 0.5))
    row_scale = jnp.repeat(spread, BLOCK, axis=0, total_repeat_length=NODES)
    base = jnp.clip(jax.random.normal(jax.random.fold_in(key, 2), (NODES, F), jnp.float32), -4.0, 4.0)
    return (base * row_scale).astype(jnp.bfloat16)


def draw_w_self(key, part):
    key = jax.random.fold_in(key, 41)
    noise = jnp.clip(jax.random.normal(jax.random.fold_in(key, 2), (F, F), jnp.float32), -4.0, 4.0)
    return signed_diagonal(key, noise, 0.25)


def draw_w_neigh(key, part):
    key = jax.random.fold_in(key, 53)
    noise = jnp.clip(jax.random.normal(jax.random.fold_in(key, 2), (F, F), jnp.float32), -4.0, 4.0)
    return signed_diagonal(key, noise, 0.25)


def draw_tile_live(key, part):
    key = jax.random.fold_in(key, 11)
    rows_idx = jnp.arange(N_ROW, dtype=jnp.int32)[:, None]
    cols_idx = jnp.arange(N_ROW, dtype=jnp.int32)[None, :]
    distance = jnp.abs(rows_idx - cols_idx)
    distance = jnp.minimum(distance, N_ROW - distance)
    threshold = jnp.where(distance == 0, 100, jnp.where(distance <= 2, 60, 15))
    rolled = jax.random.randint(key, (N_ROW, N_ROW), 0, 100)
    return (rolled < threshold).astype(jnp.int32)


def draw_pos_pairs(key, part):
    key = jax.random.fold_in(key, 21)
    return pair_table(key)


def draw_neg_pairs(key, part):
    key = jax.random.fold_in(key, 37)
    return pair_table(key)


def levels(rng, dims, pieces, smallest, largest):
    level = 1.0
    for axis_at, blocks in pieces:
        heights = jax.random.uniform(jax.random.fold_in(jax.random.fold_in(rng, 6), axis_at), (blocks,), jnp.float32, smallest / len(pieces), largest / len(pieces))
        level = level * jnp.repeat(jnp.exp(heights), dims[axis_at] // blocks).reshape((-1,) + (1,) * (len(dims) - 1 - axis_at))
    return level


def bell_draw(own_key, extent, scale, bound, pieces=(), kind=jnp.bfloat16):
    array = jax.random.normal(own_key, extent, jnp.float32) * scale
    if len(pieces) > 0:
        array = levels(own_key, extent, pieces, -0.22, 0.18) * array
    return jnp.clip(array, min=-bound, max=bound).astype(kind)


def setup_inputs(seed: int = 0) -> dict:
    streams_of = jax.random.split(jax.random.key(seed), 9)
    features = draw_features(jax.random.fold_in(streams_of[8], 71), 0)
    adjacency = bell_draw(streams_of[1], (NODES, NODES), (8 * BLOCK) ** -0.5, 0.078125, ((0, 32), (1, 8)))
    tile_live = draw_tile_live(jax.random.fold_in(streams_of[8], 71), 0)
    w_self = draw_w_self(jax.random.fold_in(streams_of[8], 71), 0)
    w_neigh = draw_w_neigh(jax.random.fold_in(streams_of[8], 71), 0)
    bias_vector = bell_draw(streams_of[5], (F,), 0.5, 3.0, (), jnp.float32)
    pos_pairs = draw_pos_pairs(jax.random.fold_in(streams_of[8], 71), 0)
    neg_pairs = draw_neg_pairs(jax.random.fold_in(streams_of[8], 71), 0)
    return {"features": features, "adjacency": adjacency, "tile_live": tile_live, "w_self": w_self, "w_neigh": w_neigh, "bias_vector": bias_vector, "pos_pairs": pos_pairs, "neg_pairs": neg_pairs}


def reference(features, adjacency, tile_live, w_self, w_neigh, bias_vector, pos_pairs, neg_pairs):

    def aggregate(row_idx):
        tile_rows = lax.dynamic_slice_in_dim(adjacency, row_idx * BLOCK, BLOCK, 0)
        flags = lax.dynamic_index_in_dim(tile_live, row_idx, 0, keepdims=False)
        col_flags = jnp.repeat(flags, BLOCK).astype(adjacency.dtype)
        return jnp.dot(tile_rows * col_flags[None, :], features, preferred_element_type=jnp.float32)
    neighbour = lax.map(aggregate, jnp.arange(N_ROW, dtype=jnp.int32)).reshape(NODES, F)
    projected = jnp.dot(features, w_self, preferred_element_type=jnp.float32)
    projected = projected + jnp.dot(neighbour.astype(jnp.bfloat16), w_neigh, preferred_element_type=jnp.float32)
    projected = projected + bias_vector.astype(jnp.float32)
    scaled = projected * lax.rsqrt(lax.optimization_barrier(jnp.mean(projected * projected, axis=-1, keepdims=True)) + 1e-06)
    embedding = scaled.astype(jnp.bfloat16)
    blocked = embedding.reshape(N_ROW, BLOCK, F)
    zero_index = jnp.zeros((), jnp.int32)

    def losses_for(pairs, direction):

        def one_row(inputs):
            row_idx, row_pairs = inputs
            query_tiles = blocked[row_idx].reshape(BLOCK // PAIR_ROWS, PAIR_ROWS, F)
            queries = query_tiles[row_pairs[:, 0]]
            replica_idx = (jnp.arange(N_REP * PAIRS, dtype=jnp.int32) // PAIRS).astype(jnp.int32)
            key_block = (replica_idx * (N_ROW // N_REP) + row_pairs[:, 1]).astype(jnp.int32)

            def take_keys(block_id, offset):
                return lax.dynamic_slice(blocked, (block_id, offset, zero_index), (1, PAIR_ROWS, F))[0]
            key_rows = jax.vmap(take_keys)(key_block, row_pairs[:, 2].astype(jnp.int32))
            scores = jnp.einsum('pqf,pkf->pqk', queries.astype(jnp.float32), key_rows.astype(jnp.float32)) / math.sqrt(F)
            return lax.optimization_barrier(jnp.mean(jax.nn.softplus(direction * scores), axis=-1))
        return lax.map(one_row, (jnp.arange(N_ROW, dtype=jnp.int32), pairs))
    pos_loss = losses_for(pos_pairs, -1.0)
    neg_loss = losses_for(neg_pairs, 1.0)
    return (embedding, pos_loss, neg_loss)
```

```python
import functools

import jax
import jax.numpy as jnp
from jax import lax
from jax.experimental import pallas as pl
from jax.experimental.pallas import tpu as pltpu
from jax.sharding import PartitionSpec as P

MESH = pl.DeviceIdType.MESH
N_Z, N_X, N_C, N_Y = 8, 4, 2, 2
N_REP = N_X * N_Y
TILE = 128
PART_TYPE = jnp.bfloat16


class Place:
    def __init__(self, yh, z, c, yl, x):
        self.yh, self.z, self.c, self.yl, self.x = yh, z, c, yl, x

    def moved(self, **kw):
        at = dict(self.__dict__)
        at.update(kw)
        return Place(**at)

    @property
    def device(self):
        return {
            "row": self.yh * (N_Z * N_C) + self.z * N_C + self.c,
            "rep": self.yl * N_X + self.x,
        }


def remote(src, dst, send_sem, recv_sem, place):
    return pltpu.make_async_remote_copy(
        src_ref=src, dst_ref=dst, send_sem=send_sem, recv_sem=recv_sem,
        device_id=place.device, device_id_type=MESH,
    )


class Spread:
    def __init__(self, me, piece, src, mid, full, sems):
        self.me, self.piece, self.src, self.mid, self.full = me, piece, src, mid, full
        self.s1, self.r1, self.s2, self.r2, self.s3, self.r3 = sems

    def rows(self, j, yl, c):
        block = (j % 2) * N_C + c
        at = block * (N_REP * self.piece) + (yl * N_X + j // 2) * self.piece
        return pl.ds(pl.multiple_of(at, 16), self.piece)

    def mid_rows(self, j):
        return pl.ds(pl.multiple_of(j * self.piece, 16), self.piece)

    def first(self, i):
        me = self.me
        d = (3 * i + 2 * me.x) % N_Z
        to = me.moved(z=(me.z + d) % N_Z, x=me.z // 2)
        stays = jnp.logical_and(d == 0, me.x == me.z // 2)
        j = me.x * 2 + me.z % 2
        copy = remote(self.src, self.mid.at[self.mid_rows(j), :], self.s1.at[i], self.r1.at[j], to)
        keep = pltpu.make_async_copy(self.src, self.mid.at[self.mid_rows(j), :], self.r1.at[j])
        return copy, keep, stays

    def start(self):
        for i in range(N_Z):
            copy, keep, stays = self.first(i)
            pl.when(stays)(keep.start)
            pl.when(jnp.logical_not(stays))(copy.start)

    def expected(self, t):
        me = self.me
        return (me.z + 2 * N_Z * 4 - 2 * me.x - 3 * t) % N_Z

    def second(self, j):
        me = self.me
        src = self.mid.at[self.mid_rows(j), :]
        dst = self.full.at[self.rows(j, me.yl, me.c), :]
        recv = self.r2.at[me.yl, j]
        far = remote(src, dst, self.s2.at[0, j], recv, me.moved(yh=1 - me.yh, yl=me.yh))
        near = remote(src, dst, self.s2.at[1, j], recv, me.moved(yl=me.yh))
        keep = pltpu.make_async_copy(src, dst, recv)
        return far, near, keep, me.yl == me.yh

    def relay(self, t):
        j = self.expected(t)
        arrived = self.mid.at[self.mid_rows(j), :]
        pltpu.make_async_copy(arrived, arrived, self.r1.at[j]).wait()
        far, near, keep, stays = self.second(j)
        far.start()
        pl.when(stays)(keep.start)
        pl.when(jnp.logical_not(stays))(near.start)

    def third(self, j, yl):
        me = self.me
        rows = self.full.at[self.rows(j, yl, me.c), :]
        return remote(rows, rows, self.s3.at[yl, j], self.r3.at[yl, j], me.moved(c=1 - me.c))

    def share(self, t):
        j = self.expected(t)
        for yl in range(N_Y):
            rows = self.full.at[self.rows(j, yl, self.me.c), :]
            pltpu.make_async_copy(rows, rows, self.r2.at[yl, j]).wait()
            self.third(j, yl).start()

    def wait_sibling(self, j):
        for yl in range(N_Y):
            rows = self.full.at[self.rows(j, yl, 1 - self.me.c), :]
            pltpu.make_async_copy(rows, rows, self.r3.at[yl, j]).wait()

    def finish(self):
        for i in range(N_Z):
            copy, _, stays = self.first(i)
            pl.when(jnp.logical_not(stays))(copy.wait_send)
        for j in range(N_Z):
            far, near, _, stays = self.second(j)
            far.wait_send()
            pl.when(jnp.logical_not(stays))(near.wait_send)
            for yl in range(N_Y):
                self.third(j, yl).wait_send()


LAG = 3


def kernel(
    live_ref, feat_ref, adj_ref, w_self_ref, w_neigh_ref, bias_ref, pos_ref, neg_ref,
    emb_ref, pos_loss_ref, neg_loss_ref,
    adj, mid_f, full_f, acc, part, got, own, mid_k, full_k, query, window, sums,
    adj_sem, f1s, f1r, f2s, f2r, f3s, f3r, k1s, k1r, k2s, k2r, k3s, k3r, ps, pr, qs, qr,
):
    row, rep = lax.axis_index("row"), lax.axis_index("rep")
    me = Place(row // (N_Z * N_C), (row // N_C) % N_Z, row % N_C, rep // N_X, rep % N_X)
    block, channels = feat_ref.shape
    piece = block // N_REP
    lists = pos_ref.shape[0]

    load = pltpu.make_async_copy(adj_ref, adj, adj_sem)
    load.start()

    barrier = pltpu.get_barrier_semaphore()

    def greet(place):
        pl.semaphore_signal(barrier, inc=1, device_id=place.device, device_id_type=MESH)

    for x in range(N_X):
        for zz in range(2):
            z = 2 * me.x + zz
            itself = jnp.logical_and(x == me.x, z == me.z)
            pl.when(jnp.logical_not(itself))(
                functools.partial(greet, me.moved(x=x, z=z))
            )
    for d in range(1, 4):
        y = (2 * me.yh + me.yl + d) % 4
        greet(me.moved(yh=y // 2, yl=y % 2))
    for d in range(1, N_REP):
        s = (rep + d) % N_REP
        greet(me.moved(yl=s // N_X, x=s % N_X))
    greet(me.moved(c=1 - me.c))
    targets = N_Z - (me.x == me.z // 2).astype(jnp.int32)
    pl.semaphore_wait(barrier, targets + 3 + (N_REP - 1) + 1)

    own_rows = pl.ds(pl.multiple_of(rep * piece, 16), piece)
    feats = Spread(me, piece, feat_ref.at[own_rows, :], mid_f, full_f, (f1s, f1r, f2s, f2r, f3s, f3r))
    feats.start()

    for section in range(4):
        column = lax.broadcasted_iota(jnp.int32, (lists, block), 1)
        for at, table in ((0, pos_ref), (lists, neg_ref)):
            first = jnp.where(table[:, 1:2] == section, table[:, 2:3], -block)
            inside = jnp.logical_and(column >= first, column < first + TILE)
            window[section, at : at + lists, :] = jnp.where(inside, 1.0, 0.0).astype(jnp.bfloat16)

    for t in range(N_Z + LAG):
        if t < N_Z:
            feats.relay(t)
        if t >= LAG:
            feats.share(t - LAG)

    load.wait()
    acc[...] = jnp.zeros_like(acc)

    def add_block(zz, c):
        k = zz * N_C + c
        at = pl.ds(pl.multiple_of(k * block, block), block)
        live = (live_ref[0, k] > 0).astype(jnp.float32).astype(jnp.bfloat16)
        acc[...] += jnp.dot(
            adj[:, at], full_f[at, :] * live, preferred_element_type=jnp.float32
        )

    for zz in range(2):
        add_block(zz, me.c)
    for zz in range(2):
        for x in range(N_X):
            feats.wait_sibling(x * 2 + zz)
        add_block(zz, 1 - me.c)

    part[...] = acc[...].astype(part.dtype)

    def partial_to(d):
        s = (rep + d) % N_REP
        return remote(
            part.at[pl.ds(pl.multiple_of(s * piece, 16), piece), :],
            got.at[d - 1], ps.at[d - 1], pr.at[d - 1], me.moved(yl=s // N_X, x=s % N_X),
        )

    for d in range(1, N_REP):
        partial_to(d).start()
    projected = jnp.dot(feat_ref[own_rows, :], w_self_ref[...], preferred_element_type=jnp.float32)
    neighbour = acc[own_rows, :]
    for d in range(1, N_REP):
        partial_to(d).wait_recv()
        neighbour = neighbour + got[d - 1].astype(jnp.float32)
    projected = projected + jnp.dot(
        neighbour.astype(jnp.bfloat16), w_neigh_ref[...], preferred_element_type=jnp.float32
    )
    projected = projected + bias_ref[...]
    scaled = projected * lax.rsqrt(jnp.mean(projected * projected, axis=-1, keepdims=True) + 1e-06)
    own[...] = scaled.astype(jnp.bfloat16)
    emb_ref[...] = own[...]

    def query_to(d):
        s = (rep + d) % N_REP
        return remote(
            own, query.at[own_rows, :], qs.at[d - 1], qr.at[d - 1], me.moved(yl=s // N_X, x=s % N_X)
        )

    keys = Spread(me, piece, own, mid_k, full_k, (k1s, k1r, k2s, k2r, k3s, k3r))
    keys.start()
    for d in range(1, N_REP):
        query_to(d).start()
    query[own_rows, :] = own[...]

    for t in range(N_Z + LAG):
        if t < N_Z:
            keys.relay(t)
        if t >= LAG:
            keys.share(t - LAG)
    for d in range(1, N_REP):
        query_to(d).wait_recv()

    sums[...] = jnp.zeros_like(sums)
    step = 2 * TILE

    def score_block(zz, c):
        k = zz * N_C + c
        for m in range(0, block, step):
            at = pl.ds(pl.multiple_of(k * block + m, step), step)
            scores = lax.dot_general(
                full_k[at, :], query[...], (((1,), (1,)), ((), ())),
                preferred_element_type=jnp.float32,
            ) * (channels ** -0.5)
            tail = jnp.log1p(jnp.exp(-jnp.abs(scores)))
            down = (tail + jnp.maximum(-scores, 0.0)).astype(jnp.bfloat16)
            up = (tail + jnp.maximum(scores, 0.0)).astype(jnp.bfloat16)
            sums[:lists, :] += jnp.dot(
                window[k, :lists, m : m + step], down, preferred_element_type=jnp.float32
            )
            sums[lists:, :] += jnp.dot(
                window[k, lists:, m : m + step], up, preferred_element_type=jnp.float32
            )

    for zz in range(2):
        score_block(zz, me.c)
    for zz in range(2):
        for x in range(N_X):
            keys.wait_sibling(x * 2 + zz)
        score_block(zz, 1 - me.c)

    for at, table, out_ref in ((0, pos_ref, pos_loss_ref), (lists, neg_ref, neg_loss_ref)):
        loss = jnp.zeros((lists, TILE), jnp.float32)
        for q in range(block // TILE):
            tile = sums[at : at + lists, q * TILE : (q + 1) * TILE]
            loss = jnp.where(table[:, 0:1] == q, tile, loss)
        out_ref[...] = loss * (1.0 / TILE)

    feats.finish()
    keys.finish()
    for d in range(1, N_REP):
        partial_to(d).wait_send()
        query_to(d).wait_send()


def per_device(features, adjacency, tile_live, w_self, w_neigh, bias_vector, pos_pairs, neg_pairs):
    block, channels = features.shape
    sources = adjacency.shape[1]
    piece = block // N_REP
    lists = pos_pairs.shape[1]
    vmem = pl.BlockSpec(memory_space=pltpu.VMEM)
    dma = pltpu.SemaphoreType.DMA
    spread_sems = [dma((N_Z,)), dma((N_Z,)), dma((2, N_Z)), dma((2, N_Z)), dma((2, N_Z)), dma((2, N_Z))]
    bf16 = jnp.bfloat16
    embedding, pos_loss, neg_loss = pl.pallas_call(
        kernel,
        out_shape=(
            jax.ShapeDtypeStruct((piece, channels), bf16),
            jax.ShapeDtypeStruct((lists, TILE), jnp.float32),
            jax.ShapeDtypeStruct((lists, TILE), jnp.float32),
        ),
        in_specs=[
            pl.BlockSpec(memory_space=pltpu.SMEM), vmem, pl.BlockSpec(memory_space=pl.ANY),
            vmem, vmem, vmem, vmem, vmem,
        ],
        out_specs=(vmem, vmem, vmem),
        scratch_shapes=[
            pltpu.VMEM((block, sources), bf16),
            pltpu.VMEM((N_Z * piece, channels), bf16),
            pltpu.VMEM((sources, channels), bf16),
            pltpu.VMEM((block, channels), jnp.float32),
            pltpu.VMEM((block, channels), PART_TYPE),
            pltpu.VMEM((N_REP - 1, piece, channels), PART_TYPE),
            pltpu.VMEM((piece, channels), bf16),
            pltpu.VMEM((N_Z * piece, channels), bf16),
            pltpu.VMEM((sources, channels), bf16),
            pltpu.VMEM((block, channels), bf16),
            pltpu.VMEM((4, 2 * lists, block), bf16),
            pltpu.VMEM((2 * lists, block), jnp.float32),
            dma(()),
            *spread_sems,
            *spread_sems,
            dma((N_REP - 1,)), dma((N_REP - 1,)), dma((N_REP - 1,)), dma((N_REP - 1,)),
        ],
        compiler_params=pltpu.CompilerParams(
            collective_id=0, has_side_effects=True, vmem_limit_bytes=40 * 1024 * 1024
        ),
    )(
        tile_live, features, adjacency, w_self, w_neigh, bias_vector.reshape(1, channels),
        pos_pairs[0], neg_pairs[0],
    )
    return embedding, pos_loss[None], neg_loss[None]


def solution(mesh):
    return jax.shard_map(
        per_device,
        mesh=mesh,
        in_specs=(
            P("row", None),
            P("row", "rep"),
            P("row", "rep"),
            P(),
            P(),
            P(),
            P("row", "rep", None),
            P("row", "rep", None),
        ),
        out_specs=(P(("row", "rep"), None), P("row", "rep", None), P("row", "rep", None)),
        check_vma=False,
    )
```

```python
import functools

import jax
import jax.numpy as jnp
from jax import lax
from jax.experimental import pallas as pl
from jax.experimental.pallas import tpu as pltpu
from jax.sharding import PartitionSpec as P

MESH = pl.DeviceIdType.MESH
N_Z, N_X, N_C, N_Y = 8, 4, 2, 2
N_REP = N_X * N_Y
TILE = 128
PART_TYPE = jnp.bfloat16


class Place:
    def __init__(self, yh, z, c, yl, x):
        self.yh, self.z, self.c, self.yl, self.x = yh, z, c, yl, x

    def moved(self, **kw):
        at = dict(self.__dict__)
        at.update(kw)
        return Place(**at)

    @property
    def device(self):
        return {
            "row": self.yh * (N_Z * N_C) + self.z * N_C + self.c,
            "rep": self.yl * N_X + self.x,
        }


def remote(src, dst, send_sem, recv_sem, place):
    return pltpu.make_async_remote_copy(
        src_ref=src, dst_ref=dst, send_sem=send_sem, recv_sem=recv_sem,
        device_id=place.device, device_id_type=MESH,
    )


def arrived(ref, sem):
    pltpu.make_async_copy(ref, ref, sem).wait()


class Spread:
    HOPS = [(dz, other) for other in (1, 0) for dz in (2, 1, -1, 0)]

    def __init__(self, me, piece, src, mirror, full, sems):
        self.me, self.piece, self.src, self.mirror, self.full = me, piece, src, mirror, full
        self.s1, self.r1, self.s2, self.r2, self.s3, self.r3 = sems

    def unit(self, zz, c, yl):
        rows = N_X * self.piece
        at = ((zz * N_C + c) * N_Y + yl) * rows
        return self.full.at[pl.ds(pl.multiple_of(at, TILE), rows), :]

    def slot(self, zz, yl, x):
        at = (((zz * N_C + self.me.c) * N_Y + yl) * N_X + x) * self.piece
        return self.full.at[pl.ds(pl.multiple_of(at, 16), self.piece), :]

    def plane(self, source, dz):
        return (source + N_Z + dz * (1 - 2 * self.me.c)) % N_Z

    def to_mirror(self):
        me = self.me
        return remote(self.src, self.mirror, self.s1, self.r1, me.moved(z=(me.z + 4) % N_Z))

    def copies(self, relayed):
        me = self.me
        source = (me.z + 4 * relayed) % N_Z
        src = self.mirror if relayed else self.src
        dst = self.slot(source % 2, me.yl, me.x)
        recv = self.r2.at[(source % 2), me.yl, me.x]
        for i, (dz, other) in enumerate(self.HOPS):
            to = me.moved(
                x=source // 2, yl=me.yh, yh=1 - me.yh if other else me.yh, z=self.plane(me.z, dz)
            )
            copy = remote(src, dst, self.s2.at[relayed, i], recv, to)
            if dz == 0 and not other:
                stays = jnp.logical_and(me.x == source // 2, me.yl == me.yh)
                yield copy, pltpu.make_async_copy(src, dst, recv), stays
            else:
                yield copy, None, None

    def send(self, relayed):
        for copy, keep, stays in self.copies(relayed):
            if keep is None:
                copy.start()
            else:
                pl.when(stays)(keep.start)
                pl.when(jnp.logical_not(stays))(copy.start)

    def start(self):
        self.to_mirror().start()
        self.send(0)

    def relay(self):
        self.to_mirror().wait_recv()
        self.send(1)

    def away(self, source, c):
        dz = (self.me.z + N_Z - source) % N_Z
        return jnp.where(c == 0, dz, (N_Z - dz) % N_Z)

    @staticmethod
    def direct(away):
        return jnp.logical_or(away <= 2, away == N_Z - 1)

    def order(self, i, c):
        first = jnp.where(self.direct(self.away(2 * self.me.x, c)), 0, 1)
        return jnp.where(i < 2, first, 1 - first), i % 2

    def to_sibling(self, zz, yl):
        me = self.me
        rows = self.unit(zz, me.c, yl)
        return remote(rows, rows, self.s3.at[zz, yl], self.r3.at[zz, yl], me.moved(c=1 - me.c))

    def take_own(self, zz, yl):
        for x in range(N_X):
            arrived(self.slot(zz, yl, x), self.r2.at[zz, yl, x])
        self.to_sibling(zz, yl).start()

    def take_sibling(self, zz, yl):
        arrived(self.unit(zz, 1 - self.me.c, yl), self.r3.at[zz, yl])

    def finish(self):
        self.to_mirror().wait_send()
        for relayed in range(2):
            for copy, keep, stays in self.copies(relayed):
                if keep is None:
                    copy.wait_send()
                else:
                    pl.when(jnp.logical_not(stays))(copy.wait_send)
        for zz in range(2):
            for yl in range(N_Y):
                self.to_sibling(zz, yl).wait_send()

    def greet(self, greet):
        me = self.me
        greet(me.moved(z=(me.z + 4) % N_Z))
        for zz in range(2):
            source = 2 * me.x + zz
            dz = self.away(source, me.c)
            z = jnp.where(self.direct(dz), source, (source + 4) % N_Z)
            for yl in range(N_Y):
                for x in range(N_X):
                    itself = jnp.logical_and(
                        jnp.logical_and(x == me.x, yl == me.yl),
                        jnp.logical_and(z == me.z, me.yh == me.yl),
                    )
                    pl.when(jnp.logical_not(itself))(
                        functools.partial(greet, me.moved(x=x, z=z, yl=yl, yh=me.yl))
                    )
        targets = 1
        for relayed in range(2):
            source = (me.z + 4 * relayed) % N_Z
            stays = jnp.logical_and(me.x == source // 2, me.yl == me.yh)
            targets = targets + len(self.HOPS) - stays.astype(jnp.int32)
        return targets


def each_unit(spread, work):
    def take(p, n):
        own = jnp.logical_or(p < 2, jnp.logical_or(p == 3, p == 5))
        i = jnp.where(own, (p + 1) // 2, (p - 1) // 2)
        i = jnp.where(p == 7, 3, i)
        c = jnp.where(own, spread.me.c, 1 - spread.me.c)
        zz, yl = spread.order(i, c)
        pl.when(own)(lambda: spread.take_own(zz, yl))
        pl.when(jnp.logical_not(own))(lambda: spread.take_sibling(zz, yl))
        work(zz, c, yl, n)

    def step(p, carry):
        take(2 * p, 0)
        take(2 * p + 1, 1)
        return carry

    lax.fori_loop(0, 4, step, 0)


def kernel(
    live_ref, feat_ref, adj_ref, w_self_ref, w_neigh_ref, bias_ref, pos_ref, neg_ref,
    emb_ref, loss_ref,
    adj, feat, w_self, w_neigh, bias, tables, live, picks,
    mirror_f, full_f, acc, part, got, own, mirror_k, full_k, query, query_t, window, down_0, up_0, down_1, up_1, last, sums,
    losses, load_sem, store_sem, f1s, f1r, f2s, f2r, f3s, f3r, k1s, k1r, k2s, k2r, k3s, k3r, ps, pr, qs, qr,
):
    row, rep = lax.axis_index("row"), lax.axis_index("rep")
    me = Place(row // (N_Z * N_C), (row // N_C) % N_Z, row % N_C, rep // N_X, rep % N_X)
    block, channels = feat_ref.shape
    piece = block // N_REP
    lists = pos_ref.shape[2]
    own_rows = pl.ds(pl.multiple_of(rep * piece, 16), piece)
    loads = [
        pltpu.make_async_copy(src, dst, load_sem.at[i])
        for i, (src, dst) in enumerate((
            (feat_ref.at[own_rows, :], feat), (pos_ref, tables.at[0]), (neg_ref, tables.at[1]),
            (live_ref, live), (adj_ref, adj),
            (w_self_ref, w_self), (w_neigh_ref, w_neigh), (bias_ref, bias),
        ))
    ]
    for load in loads:
        load.start()
    feats = Spread(me, piece, feat, mirror_f, full_f, (f1s, f1r, f2s, f2r, f3s, f3r))
    keys = Spread(me, piece, own, mirror_k, full_k, (k1s, k1r, k2s, k2r, k3s, k3r))
    pending = []

    barrier = pltpu.get_barrier_semaphore()

    def greet(place):
        pl.semaphore_signal(barrier, inc=1, device_id=place.device, device_id_type=MESH)

    targets = feats.greet(greet)
    for d in range(1, N_REP):
        s = (rep + d) % N_REP
        greet(me.moved(yl=s // N_X, x=s % N_X))
    greet(me.moved(c=1 - me.c))
    loads[0].wait()
    pl.semaphore_wait(barrier, targets + (N_REP - 1) + 1)

    feats.start()

    def down_rows(row):
        wide = jnp.broadcast_to(row, (row.shape[1], row.shape[1]))
        return jnp.transpose(wide.astype(jnp.float32)).astype(jnp.int32)

    for load in loads[1:3]:
        load.wait()
    column = lax.broadcasted_iota(jnp.int32, (lists, TILE), 1)
    for half in range(2):
        at = half * lists
        picks[at : at + lists, :] = down_rows(tables[half, 0])
        first = down_rows(tables[half, 1] * block + tables[half, 2])

        def fill(i, carry):
            for j in range(0, window.shape[2], TILE):
                since = column + (i * window.shape[2] + j) - first
                inside = jnp.logical_and(since >= 0, since < TILE)
                window[i, at : at + lists, j : j + TILE] = jnp.where(inside, 1.0, 0.0).astype(
                    jnp.bfloat16
                )
            return carry

        lax.fori_loop(0, window.shape[0], fill, 0)
    acc[...] = jnp.zeros_like(acc)
    sums[...] = jnp.zeros_like(sums)

    feats.relay()
    for load in loads[3:]:
        load.wait()

    half_block = N_X * piece

    def aggregate(zz, c, yl, n):
        k = zz * N_C + c
        flag = (live[0, k] > 0).astype(jnp.float32).astype(jnp.bfloat16)
        at = pl.ds(pl.multiple_of(k * block + yl * half_block, TILE), half_block)
        acc[...] += jnp.dot(
            adj[:, at], full_f[at, :] * flag, preferred_element_type=jnp.float32
        )

    each_unit(feats, aggregate)
    pending.append(feats.finish)

    part[...] = acc[...].astype(part.dtype)

    def partial_to(d):
        s = (rep + d) % N_REP
        return remote(
            part.at[pl.ds(pl.multiple_of(s * piece, 16), piece), :],
            got.at[d - 1], ps.at[d - 1], pr.at[d - 1], me.moved(yl=s // N_X, x=s % N_X),
        )

    for d in range(1, N_REP):
        partial_to(d).start()
    pending.extend(partial_to(d).wait_send for d in range(1, N_REP))
    projected = jnp.dot(feat[...], w_self[...], preferred_element_type=jnp.float32)
    neighbour = acc[own_rows, :]
    for d in range(1, N_REP):
        partial_to(d).wait_recv()
        neighbour = neighbour + got[d - 1].astype(jnp.float32)
    projected = projected + jnp.dot(
        neighbour.astype(jnp.bfloat16), w_neigh[...], preferred_element_type=jnp.float32
    )
    projected = projected + bias[...]
    scaled = projected * lax.rsqrt(jnp.mean(projected * projected, axis=-1, keepdims=True) + 1e-06)
    own[...] = scaled.astype(jnp.bfloat16)

    def query_to(d):
        s = (rep + d) % N_REP
        return remote(
            own, query.at[own_rows, :], qs.at[d - 1], qr.at[d - 1], me.moved(yl=s // N_X, x=s % N_X)
        )

    keys.start()
    for d in range(1, N_REP):
        query_to(d).start()
    pending.extend(query_to(d).wait_send for d in range(1, N_REP))
    query[own_rows, :] = own[...]
    store_emb = pltpu.make_async_copy(own, emb_ref, store_sem.at[0])
    store_emb.start()
    pending.append(store_emb.wait)

    keys.relay()
    for d in range(1, N_REP):
        query_to(d).wait_recv()
    scale = channels ** -0.5
    query_t[...] = (jnp.transpose(query[...].astype(jnp.float32)) * scale).astype(jnp.bfloat16)


    soft = ((down_0, up_0), (down_1, up_1))

    def add_windows(down, up):
        unit = last[0]
        rows = window[unit]
        sums[:lists, :] += jnp.dot(rows[:lists], down[...], preferred_element_type=jnp.float32)
        sums[lists:, :] += jnp.dot(rows[lists:], up[...], preferred_element_type=jnp.float32)

    def score(zz, c, yl, n):
        unit = (zz * N_C + c) * N_Y + yl
        add_windows(*soft[1 - n])
        down, up = soft[n]
        for j in range(half_block // TILE):
            at = pl.ds(pl.multiple_of(unit * half_block + j * TILE, TILE), TILE)
            rows = slice(j * TILE, (j + 1) * TILE)
            t = jnp.dot(full_k[at, :], query_t[...], preferred_element_type=jnp.float32)
            low, high = jnp.minimum(t, 0.0), jnp.maximum(t, 0.0)
            e = jnp.exp(low - high)
            tail = jnp.where(e < 2.0 ** -12, e, jnp.log(1.0 + e))
            down[rows, :] = (tail - low).astype(jnp.bfloat16)
            up[rows, :] = (tail + high).astype(jnp.bfloat16)
        last[0] = unit

    for ref in soft[1]:
        ref[...] = jnp.zeros_like(ref)
    last[0] = 0
    each_unit(keys, score)
    add_windows(*soft[1])
    pending.append(keys.finish)

    for half in range(2):
        at = half * lists
        loss = jnp.zeros((lists, TILE), jnp.float32)
        for q in range(block // TILE):
            tile = sums[at : at + lists, q * TILE : (q + 1) * TILE]
            loss = jnp.where(picks[at : at + lists, :] == q, tile, loss)
        losses[half] = loss * (1.0 / TILE)
    store_loss = pltpu.make_async_copy(losses, loss_ref, store_sem.at[1])
    store_loss.start()
    pending.append(store_loss.wait)
    for wait in pending:
        wait()


def hand_out(emb_in, loss_in, emb_ref, pos_ref, neg_ref):
    emb_ref[...] = emb_in[...]
    pos_ref[...] = loss_in[0]
    neg_ref[...] = loss_in[1]


def per_device(features, adjacency, tile_live, w_self, w_neigh, bias_vector, pos_pairs, neg_pairs):
    block, channels = features.shape
    sources = adjacency.shape[1]
    piece = block // N_REP
    lists = pos_pairs.shape[1]
    table = (pos_pairs.shape[2], 1, lists)
    place = pl.BlockSpec(memory_space=pl.ANY)
    vmem = pl.BlockSpec(memory_space=pltpu.VMEM)
    dma = pltpu.SemaphoreType.DMA
    spread_sems = [
        dma(()), dma(()), dma((2, 8)), dma((2, N_Y, N_X)), dma((2, N_Y)), dma((2, N_Y)),
    ]
    bf16 = jnp.bfloat16
    f32 = jnp.float32
    limit = 60 * 1024 * 1024
    embedding, losses = pl.pallas_call(
        kernel,
        out_shape=(
            jax.ShapeDtypeStruct((piece, channels), bf16),
            jax.ShapeDtypeStruct((2, lists, TILE), f32),
        ),
        in_specs=[place] * 8,
        out_specs=(place,) * 2,
        scratch_shapes=[
            pltpu.VMEM((block, sources), bf16),
            pltpu.VMEM((piece, channels), bf16),
            pltpu.VMEM((channels, channels), bf16),
            pltpu.VMEM((channels, channels), bf16),
            pltpu.VMEM((1, channels), jnp.float32),
            pltpu.VMEM((2, *table), jnp.int32),
            pltpu.SMEM((1, 4), jnp.int32),
            pltpu.VMEM((2 * lists, lists), jnp.int32),
            pltpu.VMEM((piece, channels), bf16),
            pltpu.VMEM((sources, channels), bf16),
            pltpu.VMEM((block, channels), jnp.float32),
            pltpu.VMEM((block, channels), PART_TYPE),
            pltpu.VMEM((N_REP - 1, piece, channels), PART_TYPE),
            pltpu.VMEM((piece, channels), bf16),
            pltpu.VMEM((piece, channels), bf16),
            pltpu.VMEM((sources, channels), bf16),
            pltpu.VMEM((block, channels), bf16),
            pltpu.VMEM((channels, block), bf16),
            pltpu.VMEM((8, 2 * lists, block // 2), bf16),
            *[pltpu.VMEM((block // 2, block), bf16)] * 4,
            pltpu.SMEM((1,), jnp.int32),
            pltpu.VMEM((2 * lists, block), jnp.float32),
            pltpu.VMEM((2, lists, TILE), f32),
            dma((8,)), dma((2,)),
            *spread_sems,
            *spread_sems,
            dma((N_REP - 1,)), dma((N_REP - 1,)), dma((N_REP - 1,)), dma((N_REP - 1,)),
        ],
        compiler_params=pltpu.CompilerParams(
            collective_id=0, has_side_effects=True, vmem_limit_bytes=limit
        ),
    )(
        tile_live, features, adjacency, w_self, w_neigh, bias_vector.reshape(1, channels),
        pos_pairs.transpose(2, 0, 1), neg_pairs.transpose(2, 0, 1),
    )
    embedding, pos_loss, neg_loss = pl.pallas_call(
        hand_out,
        out_shape=(
            jax.ShapeDtypeStruct((piece, channels), bf16),
            jax.ShapeDtypeStruct((lists, TILE), f32),
            jax.ShapeDtypeStruct((lists, TILE), f32),
        ),
        in_specs=[vmem] * 2,
        out_specs=(vmem,) * 3,
        compiler_params=pltpu.CompilerParams(vmem_limit_bytes=limit),
    )(embedding, losses)
    return embedding, pos_loss[None], neg_loss[None]


def solution(mesh):
    return jax.shard_map(
        per_device,
        mesh=mesh,
        in_specs=(
            P("row", None),
            P("row", "rep"),
            P("row", "rep"),
            P(),
            P(),
            P(),
            P("row", "rep", None),
            P("row", "rep", None),
        ),
        out_specs=(P(("row", "rep"), None), P("row", "rep", None), P("row", "rep", None)),
        check_vma=False,
    )
```

```python
import functools

import jax
import jax.numpy as jnp
from jax import lax
from jax.experimental import pallas as pl
from jax.experimental.pallas import tpu as pltpu
from jax.sharding import PartitionSpec as P

MESH = pl.DeviceIdType.MESH
N_Z, N_X, N_C, N_Y = 8, 4, 2, 2
N_REP = N_X * N_Y
TILE = 128
PART_TYPE = jnp.bfloat16


class Place:
    def __init__(self, yh, z, c, yl, x):
        self.yh, self.z, self.c, self.yl, self.x = yh, z, c, yl, x

    def moved(self, **kw):
        at = dict(self.__dict__)
        at.update(kw)
        return Place(**at)

    @property
    def device(self):
        return {
            "row": self.yh * (N_Z * N_C) + self.z * N_C + self.c,
            "rep": self.yl * N_X + self.x,
        }


def remote(src, dst, send_sem, recv_sem, place):
    return pltpu.make_async_remote_copy(
        src_ref=src, dst_ref=dst, send_sem=send_sem, recv_sem=recv_sem,
        device_id=place.device, device_id_type=MESH,
    )


def arrived(ref, sem):
    pltpu.make_async_copy(ref, ref, sem).wait()


class Spread:
    STEPS = (2, 1, -1, 0)

    def __init__(self, me, piece, held, full, sems):
        self.me, self.piece, self.held, self.full = me, piece, held, full
        self.s1, self.r1, self.s2, self.r2, self.s3, self.r3 = sems
        self.outer = me.yl == me.yh
        self.twin = me.moved(yh=1 - me.yh, yl=1 - me.yl)

    def unit(self, zz, c, yl):
        rows = N_X * self.piece
        at = ((zz * N_C + c) * N_Y + yl) * rows
        return self.full.at[pl.ds(pl.multiple_of(at, TILE), rows), :]

    def slot(self, zz, yl, x):
        at = (((zz * N_C + self.me.c) * N_Y + yl) * N_X + x) * self.piece
        return self.full.at[pl.ds(pl.multiple_of(at, 16), self.piece), :]

    def plane(self, source, dz):
        return (source + N_Z + dz * (1 - 2 * self.me.c)) % N_Z

    def mirrored(self):
        me, twin = self.me, self.twin
        return me.moved(
            z=(me.z + 4) % N_Z,
            yh=jnp.where(self.outer, twin.yh, me.yh), yl=jnp.where(self.outer, twin.yl, me.yl),
        )

    def to_mirror(self):
        return remote(self.held.at[0], self.held.at[2], self.s1.at[0], self.r1.at[0], self.mirrored())

    def to_twin(self):
        return remote(self.held.at[0], self.held.at[1], self.s1.at[1], self.r1.at[1], self.twin)

    def copies(self, relayed, other):
        me = self.me
        if relayed:
            owner, at = self.mirrored(), 2
        elif other:
            owner = me.moved(
                yh=jnp.where(self.outer, self.twin.yh, me.yh),
                yl=jnp.where(self.outer, self.twin.yl, me.yl),
            )
            at = self.outer.astype(jnp.int32)
        else:
            owner, at = me, 0
        src = self.held.at[at]
        dst = self.slot(owner.z % 2, owner.yl, me.x)
        recv = self.r2.at[owner.z % 2, owner.yl, me.x]
        for i, dz in enumerate(self.STEPS):
            to = me.moved(
                x=owner.z // 2, yl=owner.yh, yh=1 - owner.yh if other else owner.yh,
                z=self.plane(me.z, dz),
            )
            copy = remote(src, dst, self.s2.at[relayed, other, i], recv, to)
            if dz == 0 and not other and not relayed:
                stays = jnp.logical_and(me.x == me.z // 2, self.outer)
                yield copy, pltpu.make_async_copy(src, dst, recv), stays
            else:
                yield copy, None, None

    def send(self, relayed, other):
        for copy, keep, stays in self.copies(relayed, other):
            if keep is None:
                copy.start()
            else:
                pl.when(stays)(keep.start)
                pl.when(jnp.logical_not(stays))(copy.start)

    def start(self):
        self.to_mirror().start()
        pl.when(self.outer)(self.to_twin().start)
        self.send(0, 0)
        pl.when(self.outer)(self.to_twin().wait_recv)
        self.send(0, 1)

    def relay(self):
        self.to_mirror().wait_recv()
        self.send(1, 1)
        self.send(1, 0)

    def away(self, source, c):
        dz = (self.me.z + N_Z - source) % N_Z
        return jnp.where(c == 0, dz, (N_Z - dz) % N_Z)

    @staticmethod
    def direct(away):
        return jnp.logical_or(away <= 2, away == N_Z - 1)

    def order(self, i, c):
        first = jnp.where(self.direct(self.away(2 * self.me.x, c)), 0, 1)
        return jnp.where(i < 2, first, 1 - first), i % 2

    def to_sibling(self, zz, yl):
        me = self.me
        rows = self.unit(zz, me.c, yl)
        return remote(rows, rows, self.s3.at[zz, yl], self.r3.at[zz, yl], me.moved(c=1 - me.c))

    def take_own(self, zz, yl):
        for x in range(N_X):
            arrived(self.slot(zz, yl, x), self.r2.at[zz, yl, x])
        self.to_sibling(zz, yl).start()

    def take_sibling(self, zz, yl):
        arrived(self.unit(zz, 1 - self.me.c, yl), self.r3.at[zz, yl])

    def finish(self):
        self.to_mirror().wait_send()
        pl.when(self.outer)(self.to_twin().wait_send)
        for relayed in range(2):
            for other in range(2):
                for copy, keep, stays in self.copies(relayed, other):
                    if keep is None:
                        copy.wait_send()
                    else:
                        pl.when(jnp.logical_not(stays))(copy.wait_send)
        for zz in range(2):
            for yl in range(N_Y):
                self.to_sibling(zz, yl).wait_send()

    def greet(self, greet):
        me = self.me
        greet(self.mirrored())
        pl.when(self.outer)(functools.partial(greet, self.twin))
        for zz in range(2):
            source = 2 * me.x + zz
            dz = self.away(source, me.c)
            direct = self.direct(dz)
            z = jnp.where(direct, source, (source + 4) % N_Z)
            near = jnp.logical_and(direct, self.outer)
            swap = jnp.where(near, 0, 1)
            for x in range(N_X):
                outer = me.moved(x=x, z=z, yl=(me.yl + swap) % 2, yh=(me.yl + swap) % 2)
                itself = jnp.logical_and(jnp.logical_and(x == me.x, z == me.z), near)
                pl.when(jnp.logical_not(itself))(functools.partial(greet, outer))
                greet(me.moved(x=x, z=z, yl=1 - me.yl, yh=me.yl))
        stays = jnp.logical_and(me.x == me.z // 2, self.outer)
        return 17 + self.outer.astype(jnp.int32) - stays.astype(jnp.int32)


def each_unit(spread, work):
    def take(p, n):
        own = jnp.logical_or(p < 2, jnp.logical_or(p == 3, p == 5))
        i = jnp.where(own, (p + 1) // 2, (p - 1) // 2)
        i = jnp.where(p == 7, 3, i)
        c = jnp.where(own, spread.me.c, 1 - spread.me.c)
        zz, yl = spread.order(i, c)
        pl.when(own)(lambda: spread.take_own(zz, yl))
        pl.when(jnp.logical_not(own))(lambda: spread.take_sibling(zz, yl))
        work(zz, c, yl, n)

    def step(p, carry):
        take(2 * p, 0)
        take(2 * p + 1, 1)
        return carry

    lax.fori_loop(0, 4, step, 0)


def kernel(
    live_ref, feat_ref, adj_ref, w_self_ref, w_neigh_ref, bias_ref, pos_ref, neg_ref,
    emb_ref, loss_ref,
    adj, w_self, w_neigh, bias, tables, live,
    held_f, full_f, acc, part, got, held_k, full_k, query, scaled_query, window, soft_0, soft_1, last, sums,
    losses, load_sem, store_sem, f1s, f1r, f2s, f2r, f3s, f3r, k1s, k1r, k2s, k2r, k3s, k3r, ps, pr, qs, qr,
):
    row, rep = lax.axis_index("row"), lax.axis_index("rep")
    me = Place(row // (N_Z * N_C), (row // N_C) % N_Z, row % N_C, rep // N_X, rep % N_X)
    block, channels = feat_ref.shape
    piece = block // N_REP
    lists = pos_ref.shape[2]
    own_rows = pl.ds(pl.multiple_of(rep * piece, 16), piece)
    loads = [
        pltpu.make_async_copy(src, dst, load_sem.at[i])
        for i, (src, dst) in enumerate((
            (feat_ref.at[own_rows, :], held_f.at[0]), (pos_ref, tables.at[0]), (neg_ref, tables.at[1]),
            (live_ref, live), (adj_ref, adj),
            (w_self_ref, w_self), (w_neigh_ref, w_neigh), (bias_ref, bias),
        ))
    ]
    loads[0].start()
    feats = Spread(me, piece, held_f, full_f, (f1s, f1r, f2s, f2r, f3s, f3r))
    keys = Spread(me, piece, held_k, full_k, (k1s, k1r, k2s, k2r, k3s, k3r))
    own = held_k.at[0]
    pending = []

    barrier = pltpu.get_barrier_semaphore()

    def greet(place):
        pl.semaphore_signal(barrier, inc=1, device_id=place.device, device_id_type=MESH)

    targets = feats.greet(greet)
    for d in range(1, N_REP):
        s = (rep + d) % N_REP
        greet(me.moved(yl=s // N_X, x=s % N_X))
    greet(me.moved(c=1 - me.c))
    for load in loads[1:]:
        load.start()
    loads[0].wait()
    pl.semaphore_wait(barrier, targets + (N_REP - 1) + 1)

    feats.start()

    for load in loads[1:3]:
        load.wait()
    half_block = N_X * piece
    row_at = lax.broadcasted_iota(jnp.int32, (TILE, lists), 0)
    nothing = jnp.zeros((half_block, lists), jnp.bfloat16)
    first = [tables[half, 1] * block + tables[half, 2] for half in range(2)]

    def fill(unit, carry):
        window[unit, :half_block, lists:] = nothing
        window[unit, half_block:, :lists] = nothing
        for half in range(2):
            for j in range(0, half_block, TILE):
                since = row_at + (unit * half_block + j) - first[half]
                inside = jnp.logical_and(since >= 0, since < TILE)
                at = half * half_block + j
                window[unit, at : at + TILE, half * lists : (half + 1) * lists] = jnp.where(
                    inside, 1.0, 0.0
                ).astype(jnp.bfloat16)
        return carry

    lax.fori_loop(0, 8, fill, 0)
    acc[...] = jnp.zeros_like(acc)
    sums[...] = jnp.zeros_like(sums)

    feats.relay()
    for load in loads[3:]:
        load.wait()

    def aggregate(zz, c, yl, n):
        k = zz * N_C + c
        flag = (live[0, k] > 0).astype(jnp.float32).astype(jnp.bfloat16)
        at = pl.ds(pl.multiple_of(k * block + yl * half_block, TILE), half_block)
        acc[...] += jnp.dot(
            adj[:, at], full_f[at, :] * flag, preferred_element_type=jnp.float32
        )

    each_unit(feats, aggregate)
    pending.append(feats.finish)

    part[...] = acc[...].astype(part.dtype)

    def partial_to(d):
        s = (rep + d) % N_REP
        return remote(
            part.at[pl.ds(pl.multiple_of(s * piece, 16), piece), :],
            got.at[d - 1], ps.at[d - 1], pr.at[d - 1], me.moved(yl=s // N_X, x=s % N_X),
        )

    for d in range(1, N_REP):
        partial_to(d).start()
    pending.extend(partial_to(d).wait_send for d in range(1, N_REP))
    projected = jnp.dot(held_f[0], w_self[...], preferred_element_type=jnp.float32)
    neighbour = acc[own_rows, :]
    for d in range(1, N_REP):
        partial_to(d).wait_recv()
        neighbour = neighbour + got[d - 1].astype(jnp.float32)
    projected = projected + jnp.dot(
        neighbour.astype(jnp.bfloat16), w_neigh[...], preferred_element_type=jnp.float32
    )
    projected = projected + bias[...]
    scaled = projected * lax.rsqrt(jnp.mean(projected * projected, axis=-1, keepdims=True) + 1e-06)
    held_k[0] = scaled.astype(jnp.bfloat16)

    def query_to(d):
        x = (me.x + d) % N_X
        return remote(own, query.at[own_rows, :], qs.at[d - 1], qr.at[d - 1], me.moved(x=x))

    def query_half(yl):
        rows = query.at[pl.ds(pl.multiple_of(yl * half_block, TILE), half_block), :]
        return remote(rows, rows, qs.at[N_X - 1], qr.at[N_X - 1], me.moved(yl=1 - me.yl))

    for d in range(1, N_X):
        query_to(d).start()
    keys.start()
    query[own_rows, :] = held_k[0]
    store_emb = pltpu.make_async_copy(own, emb_ref, store_sem.at[0])
    store_emb.start()
    pending.append(store_emb.wait)
    for d in range(1, N_X):
        query_to(d).wait_recv()
    query_half(me.yl).start()
    pending.extend(query_to(d).wait_send for d in range(1, N_X))
    pending.append(query_half(me.yl).wait_send)

    keys.relay()
    query_half(1 - me.yl).wait_recv()
    scaled_query[...] = query[...] * channels ** -0.5
    soft = (soft_0, soft_1)

    def add_windows(ref):
        sums[...] += jnp.dot(ref[...], window[last[0]], preferred_element_type=jnp.float32)

    def score(zz, c, yl, n):
        unit = (zz * N_C + c) * N_Y + yl
        add_windows(soft[1 - n])
        for j in range(0, half_block, TILE):
            at = pl.ds(pl.multiple_of(unit * half_block + j, TILE), TILE)
            t = lax.dot_general(
                scaled_query[...], full_k[at, :], (((1,), (1,)), ((), ())),
                preferred_element_type=jnp.float32,
            )
            low, high = jnp.minimum(t, 0.0), jnp.maximum(t, 0.0)
            e = jnp.exp(low - high)
            tail = jnp.where(e < 2.0 ** -12, e, jnp.log(1.0 + e))
            soft[n][:, j : j + TILE] = (tail - low).astype(jnp.bfloat16)
            soft[n][:, half_block + j : half_block + j + TILE] = (tail + high).astype(jnp.bfloat16)
        last[0] = unit

    soft_1[...] = jnp.zeros_like(soft_1)
    last[0] = 0
    each_unit(keys, score)
    add_windows(soft_1)
    pending.append(keys.finish)

    for half in range(2):
        loss = jnp.zeros((TILE, lists), jnp.float32)
        for q in range(block // TILE):
            tile = sums[q * TILE : (q + 1) * TILE, half * lists : (half + 1) * lists]
            loss = jnp.where(tables[half, 0] == q, tile, loss)
        losses[half] = jnp.transpose(loss * (1.0 / TILE))
    store_loss = pltpu.make_async_copy(losses, loss_ref, store_sem.at[1])
    store_loss.start()
    pending.append(store_loss.wait)
    for wait in pending:
        wait()


def hand_out(emb_in, loss_in, emb_ref, pos_ref, neg_ref):
    emb_ref[...] = emb_in[...]
    pos_ref[...] = loss_in[0]
    neg_ref[...] = loss_in[1]


def per_device(features, adjacency, tile_live, w_self, w_neigh, bias_vector, pos_pairs, neg_pairs):
    block, channels = features.shape
    sources = adjacency.shape[1]
    piece = block // N_REP
    lists = pos_pairs.shape[1]
    table = (pos_pairs.shape[2], 1, lists)
    place = pl.BlockSpec(memory_space=pl.ANY)
    vmem = pl.BlockSpec(memory_space=pltpu.VMEM)
    dma = pltpu.SemaphoreType.DMA
    spread_sems = [
        dma((2,)), dma((2,)), dma((2, 2, 4)), dma((2, N_Y, N_X)), dma((2, N_Y)), dma((2, N_Y)),
    ]
    bf16 = jnp.bfloat16
    f32 = jnp.float32
    limit = 60 * 1024 * 1024
    embedding, losses = pl.pallas_call(
        kernel,
        out_shape=(
            jax.ShapeDtypeStruct((piece, channels), bf16),
            jax.ShapeDtypeStruct((2, lists, TILE), f32),
        ),
        in_specs=[place] * 8,
        out_specs=(place,) * 2,
        scratch_shapes=[
            pltpu.VMEM((block, sources), bf16),
            pltpu.VMEM((channels, channels), bf16),
            pltpu.VMEM((channels, channels), bf16),
            pltpu.VMEM((1, channels), f32),
            pltpu.VMEM((2, *table), jnp.int32),
            pltpu.SMEM((1, 4), jnp.int32),
            pltpu.VMEM((3, piece, channels), bf16),
            pltpu.VMEM((sources, channels), bf16),
            pltpu.VMEM((block, channels), f32),
            pltpu.VMEM((block, channels), PART_TYPE),
            pltpu.VMEM((N_REP - 1, piece, channels), PART_TYPE),
            pltpu.VMEM((3, piece, channels), bf16),
            pltpu.VMEM((sources, channels), bf16),
            pltpu.VMEM((block, channels), bf16),
            pltpu.VMEM((block, channels), bf16),
            pltpu.VMEM((8, block, 2 * lists), bf16),
            pltpu.VMEM((block, block), bf16),
            pltpu.VMEM((block, block), bf16),
            pltpu.SMEM((1,), jnp.int32),
            pltpu.VMEM((block, 2 * lists), f32),
            pltpu.VMEM((2, lists, TILE), f32),
            dma((8,)), dma((2,)),
            *spread_sems,
            *spread_sems,
            dma((N_REP - 1,)), dma((N_REP - 1,)), dma((N_X,)), dma((N_X,)),
        ],
        compiler_params=pltpu.CompilerParams(
            collective_id=0, has_side_effects=True, vmem_limit_bytes=limit
        ),
    )(
        tile_live, features, adjacency, w_self, w_neigh, bias_vector.reshape(1, channels),
        pos_pairs.transpose(2, 0, 1), neg_pairs.transpose(2, 0, 1),
    )
    embedding, pos_loss, neg_loss = pl.pallas_call(
        hand_out,
        out_shape=(
            jax.ShapeDtypeStruct((piece, channels), bf16),
            jax.ShapeDtypeStruct((lists, TILE), f32),
            jax.ShapeDtypeStruct((lists, TILE), f32),
        ),
        in_specs=[vmem] * 2,
        out_specs=(vmem,) * 3,
        compiler_params=pltpu.CompilerParams(vmem_limit_bytes=limit),
    )(embedding, losses)
    return embedding, pos_loss[None], neg_loss[None]


def solution(mesh):
    return jax.shard_map(
        per_device,
        mesh=mesh,
        in_specs=(
            P("row", None),
            P("row", "rep"),
            P("row", "rep"),
            P(),
            P(),
            P(),
            P("row", "rep", None),
            P("row", "rep", None),
        ),
        out_specs=(P(("row", "rep"), None), P("row", "rep", None), P("row", "rep", None)),
        check_vma=False,
    )
```

```python
import functools

import jax
import jax.numpy as jnp
from jax import lax
from jax.experimental import pallas as pl
from jax.experimental.pallas import tpu as pltpu
from jax.sharding import PartitionSpec as P

MESH = pl.DeviceIdType.MESH
N_Z, N_X, N_C, N_Y = 8, 4, 2, 2
N_REP = N_X * N_Y
TILE = 128
PART_TYPE = jnp.bfloat16


def mod(a, n):
    return lax.rem(a, jnp.int32(n))


def div(a, n):
    return lax.div(a, jnp.int32(n))


class Place:
    def __init__(self, yh, z, c, yl, x):
        self.yh, self.z, self.c, self.yl, self.x = yh, z, c, yl, x

    def moved(self, **kw):
        at = dict(self.__dict__)
        at.update(kw)
        return Place(**at)

    @property
    def device(self):
        return {
            "row": self.yh * (N_Z * N_C) + self.z * N_C + self.c,
            "rep": self.yl * N_X + self.x,
        }


def remote(src, dst, send_sem, recv_sem, place):
    return pltpu.make_async_remote_copy(
        src_ref=src, dst_ref=dst, send_sem=send_sem, recv_sem=recv_sem,
        device_id=place.device, device_id_type=MESH,
    )


def arrived(ref, sem):
    pltpu.make_async_copy(ref, ref, sem).wait()


class Spread:
    SHIFTS = (0, 3, -3)
    STEPS = ((1, -1, 0), (1, -1, 0), (1, 0))

    def __init__(self, me, piece, held, full, sems):
        self.me, self.piece, self.held, self.full = me, piece, held, full
        self.s1, self.r1, self.s2, self.r2, self.s3, self.r3 = sems
        self.outer = me.yl == me.yh
        self.twin = me.moved(yh=1 - me.yh, yl=1 - me.yl)
        way = 1 - 2 * me.c
        self.planes = {dz: mod(me.z + N_Z + dz * way, N_Z) for dz in (0, 1, -1, 3, -3)}
        self.side = dict(
            yh=jnp.where(self.outer, self.twin.yh, me.yh), yl=jnp.where(self.outer, self.twin.yl, me.yl)
        )
        away = mod(me.z + N_Z - 2 * me.x, N_Z)
        first = [
            jnp.where(self.direct(a), 0, 1) for a in (away, mod(N_Z - away, N_Z))
        ]
        self.first = (
            jnp.where(me.c == 0, first[0], first[1]), jnp.where(me.c == 0, first[1], first[0])
        )

    def unit(self, zz, c, yl):
        rows = N_X * self.piece
        at = ((zz * N_C + c) * N_Y + yl) * rows
        return self.full.at[pl.ds(pl.multiple_of(at, TILE), rows), :]

    def slot(self, zz, yl, x):
        at = (((zz * N_C + self.me.c) * N_Y + yl) * N_X + x) * self.piece
        return self.full.at[pl.ds(pl.multiple_of(at, 16), self.piece), :]

    def beside(self, dz):
        return self.me.moved(z=self.planes[dz], **self.side)

    def to_holder(self, k):
        return remote(
            self.held.at[0], self.held.at[1 + k], self.s1.at[k], self.r1.at[k],
            self.beside(self.SHIFTS[k]),
        )

    def to_twin(self):
        return remote(self.held.at[0], self.held.at[1], self.s1.at[0], self.r1.at[0], self.twin)

    def copies(self, k, other):
        me = self.me
        if k:
            owner, at = self.beside(-self.SHIFTS[k]), 1 + k
        elif other:
            owner, at = self.beside(0), jnp.where(self.outer, 1, 0)
        else:
            owner, at = me, 0
        src = self.held.at[at]
        zz, x = mod(owner.z, 2), div(owner.z, 2)
        dst = self.slot(zz, owner.yl, me.x)
        recv = self.r2.at[zz, owner.yl, me.x]
        for i, dz in enumerate(self.STEPS[k]):
            to = me.moved(
                x=x, yl=owner.yh, yh=1 - owner.yh if other else owner.yh,
                z=self.planes[dz],
            )
            copy = remote(src, dst, self.s2.at[k, other, i], recv, to)
            if dz == 0 and not other and not k:
                stays = jnp.logical_and(me.x == x, self.outer)
                yield copy, pltpu.make_async_copy(src, dst, recv), stays
            else:
                yield copy, None, None

    def send(self, k, other):
        for copy, keep, stays in self.copies(k, other):
            if keep is None:
                copy.start()
            else:
                pl.when(stays)(keep.start)
                pl.when(jnp.logical_not(stays))(copy.start)

    def start_holders(self):
        self.to_holder(1).start()
        self.to_holder(2).start()
        pl.when(self.outer)(self.to_twin().start)

    def start(self):
        self.send(0, 0)
        pl.when(self.outer)(self.to_twin().wait_recv)
        self.send(0, 1)

    def relay(self):
        for k in (1, 2):
            self.to_holder(k).wait_recv()
            self.send(k, 1)
            self.send(k, 0)

    def away(self, source, c):
        dz = mod(self.me.z + N_Z - source, N_Z)
        return jnp.where(c == 0, dz, mod(N_Z - dz, N_Z))

    @staticmethod
    def direct(away):
        return jnp.logical_or(away <= 1, away == N_Z - 1)

    def order(self, i, sibling):
        first = self.first[sibling]
        return jnp.where(i == 0, first, 1 - first)

    def to_sibling(self, zz, yl):
        me = self.me
        rows = self.unit(zz, me.c, yl)
        return remote(rows, rows, self.s3.at[zz, yl], self.r3.at[zz, yl], me.moved(c=1 - me.c))

    def take_own(self, zz, yl):
        for x in range(N_X):
            arrived(self.slot(zz, yl, x), self.r2.at[zz, yl, x])
        self.to_sibling(zz, yl).start()

    def take_sibling(self, zz, yl):
        arrived(self.unit(zz, 1 - self.me.c, yl), self.r3.at[zz, yl])

    def finish(self):
        self.to_holder(1).wait_send()
        self.to_holder(2).wait_send()
        pl.when(self.outer)(self.to_twin().wait_send)
        for k in range(3):
            for other in range(2):
                for copy, keep, stays in self.copies(k, other):
                    if keep is None:
                        copy.wait_send()
                    else:
                        pl.when(jnp.logical_not(stays))(copy.wait_send)
        for zz in range(2):
            for yl in range(N_Y):
                self.to_sibling(zz, yl).wait_send()

    def greet(self, greet):
        me = self.me
        greet(self.beside(3))
        greet(self.beside(-3))
        pl.when(self.outer)(functools.partial(greet, self.twin))
        for zz in range(2):
            source = 2 * me.x + zz
            away = self.away(source, me.c)
            direct = self.direct(away)
            shift = jnp.where(direct, 0, jnp.where(away <= 4, 3, N_Z - 3))
            z = mod(source + jnp.where(me.c == 0, shift, N_Z - shift), N_Z)
            near = jnp.logical_and(direct, self.outer)
            swap = jnp.where(near, 0, 1)
            for x in range(N_X):
                outer = me.moved(x=x, z=z, yl=(me.yl + swap) % 2, yh=(me.yl + swap) % 2)
                itself = jnp.logical_and(jnp.logical_and(x == me.x, z == me.z), near)
                pl.when(jnp.logical_not(itself))(functools.partial(greet, outer))
                greet(me.moved(x=x, z=z, yl=1 - me.yl, yh=me.yl))
        stays = jnp.logical_and(me.x == div(me.z, 2), self.outer)
        return 18 + jnp.where(self.outer, 1, 0) - jnp.where(stays, 1, 0)


def each_block(spread, work):
    me = spread.me

    def take_own(i):
        zz = spread.order(i, 0)
        for yl in range(N_Y):
            spread.take_own(zz, yl)
        return zz, me.c

    def take_sibling(i):
        zz = spread.order(i, 1)
        for yl in range(N_Y):
            spread.take_sibling(zz, yl)
        return zz, 1 - me.c

    def step(q, carry):
        for n in range(2):
            work(*lax.cond(q == 0, take_own, take_sibling, n), n)
        return carry

    lax.fori_loop(0, 2, step, 0)


def kernel(
    live_ref, feat_ref, adj_ref, w_self_ref, w_neigh_ref, bias_ref, pos_ref, neg_ref,
    emb_ref, loss_ref,
    adj, w_self, w_neigh, bias, tables, live,
    held_f, full_f, acc, part, got, held_k, full_k, query, scaled_query, window, soft_0, soft_1, last, sums,
    losses, load_sem, store_sem, f1s, f1r, f2s, f2r, f3s, f3r, k1s, k1r, k2s, k2r, k3s, k3r, ps, pr, qs, qr,
):
    row, rep = lax.axis_index("row"), lax.axis_index("rep")
    me = Place(div(row, N_Z * N_C), mod(div(row, N_C), N_Z), mod(row, N_C), div(rep, N_X), mod(rep, N_X))
    peers = [
        me.moved(yl=1 - me.yl if dy else me.yl, x=mod(me.x + dx, N_X))
        for dy, dx in ((1, 2), (1, 1), (1, 3), (0, 2), (0, 1), (0, 3), (1, 0))
    ]
    block, channels = feat_ref.shape
    piece = block // N_REP
    lists = pos_ref.shape[2]
    own_rows = pl.ds(pl.multiple_of(rep * piece, 16), piece)
    loads = [
        pltpu.make_async_copy(src, dst, load_sem.at[i])
        for i, (src, dst) in enumerate((
            (feat_ref.at[own_rows, :], held_f.at[0]), (pos_ref, tables.at[0]), (neg_ref, tables.at[1]),
            (live_ref, live), (adj_ref, adj),
            (w_self_ref, w_self), (w_neigh_ref, w_neigh), (bias_ref, bias),
        ))
    ]
    loads[0].start()
    feats = Spread(me, piece, held_f, full_f, (f1s, f1r, f2s, f2r, f3s, f3r))
    keys = Spread(me, piece, held_k, full_k, (k1s, k1r, k2s, k2r, k3s, k3r))
    own = held_k.at[0]
    pending = []

    barrier = pltpu.get_barrier_semaphore()

    def greet(place):
        pl.semaphore_signal(barrier, inc=1, device_id=place.device, device_id_type=MESH)

    targets = feats.greet(greet)
    for peer in peers:
        greet(peer)
    greet(me.moved(c=1 - me.c))
    for load in loads[1:]:
        load.start()
    loads[0].wait()
    pl.semaphore_wait(barrier, targets + (N_REP - 1) + 1)

    feats.start_holders()
    feats.start()

    for load in loads[1:3]:
        load.wait()
    half_block = N_X * piece
    row_at = lax.broadcasted_iota(jnp.int32, (TILE, lists), 0)
    nothing = jnp.zeros((block, lists), jnp.bfloat16)
    first = [tables[half, 1] * block + tables[half, 2] for half in range(2)]

    def fill(k, carry):
        window[k, :block, lists:] = nothing
        window[k, block:, :lists] = nothing
        for half in range(2):
            for j in range(0, block, TILE):
                since = row_at + (k * block + j) - first[half]
                inside = jnp.logical_and(since >= 0, since < TILE)
                at = half * block + j
                window[k, at : at + TILE, half * lists : (half + 1) * lists] = jnp.where(
                    inside, 1.0, 0.0
                ).astype(jnp.bfloat16)
        return carry

    lax.fori_loop(0, 4, fill, 0)
    acc[...] = jnp.zeros_like(acc)
    sums[...] = jnp.zeros_like(sums)

    feats.relay()
    for load in loads[3:]:
        load.wait()

    def aggregate(zz, c, n):
        k = zz * N_C + c
        flag = (live[0, k] > 0).astype(jnp.float32).astype(jnp.bfloat16)
        at = pl.ds(pl.multiple_of(k * block, TILE), block)
        acc[...] += jnp.dot(
            adj[:, at], full_f[at, :] * flag, preferred_element_type=jnp.float32
        )

    each_block(feats, aggregate)
    pending.append(feats.finish)

    part[...] = acc[...].astype(part.dtype)

    def partial_to(d):
        at = (peers[d].yl * N_X + peers[d].x) * piece
        return remote(
            part.at[pl.ds(pl.multiple_of(at, 16), piece), :],
            got.at[d], ps.at[d], pr.at[d], peers[d],
        )

    for d in range(N_REP - 1):
        partial_to(d).start()
    pending.extend(partial_to(d).wait_send for d in range(N_REP - 1))
    projected = jnp.dot(held_f[0], w_self[...], preferred_element_type=jnp.float32)
    neighbour = acc[own_rows, :]
    for d in range(N_REP - 1):
        partial_to(d).wait_recv()
        neighbour = neighbour + got[d].astype(jnp.float32)
    projected = projected + jnp.dot(
        neighbour.astype(jnp.bfloat16), w_neigh[...], preferred_element_type=jnp.float32
    )
    projected = projected + bias[...]
    scaled = projected * lax.rsqrt(jnp.mean(projected * projected, axis=-1, keepdims=True) + 1e-06)
    held_k[0] = scaled.astype(jnp.bfloat16)

    def query_to(d):
        x = mod(me.x + d, N_X)
        return remote(own, query.at[own_rows, :], qs.at[d - 1], qr.at[d - 1], me.moved(x=x))

    def query_half(yl):
        rows = query.at[pl.ds(pl.multiple_of(yl * half_block, TILE), half_block), :]
        return remote(rows, rows, qs.at[N_X - 1], qr.at[N_X - 1], me.moved(yl=1 - me.yl))

    keys.start_holders()
    for d in range(1, N_X):
        query_to(d).start()
    keys.start()
    query[own_rows, :] = held_k[0]
    store_emb = pltpu.make_async_copy(own, emb_ref, store_sem.at[0])
    store_emb.start()
    for wait in pending:
        wait()
    pending.clear()
    pending.append(store_emb.wait)
    for d in range(1, N_X):
        query_to(d).wait_recv()
    query_half(me.yl).start()
    pending.extend(query_to(d).wait_send for d in range(1, N_X))
    pending.append(query_half(me.yl).wait_send)

    keys.relay()
    query_half(1 - me.yl).wait_recv()
    scaled_query[...] = query[...] * channels ** -0.5
    soft = (soft_0, soft_1)

    def add_windows(ref):
        sums[...] += jnp.dot(ref[...], window[last[0]], preferred_element_type=jnp.float32)

    def score(zz, c, n):
        k = zz * N_C + c
        add_windows(soft[1 - n])
        for j in range(0, block, TILE):
            at = pl.ds(pl.multiple_of(k * block + j, TILE), TILE)
            t = lax.dot_general(
                scaled_query[...], full_k[at, :], (((1,), (1,)), ((), ())),
                preferred_element_type=jnp.float32,
            )
            low, high = jnp.minimum(t, 0.0), jnp.maximum(t, 0.0)
            e = jnp.exp(low - high)
            tail = jnp.where(e < 2.0 ** -12, e, jnp.log(1.0 + e))
            soft[n][:, j : j + TILE] = (tail - low).astype(jnp.bfloat16)
            soft[n][:, block + j : block + j + TILE] = (tail + high).astype(jnp.bfloat16)
        last[0] = k

    soft_1[...] = jnp.zeros_like(soft_1)
    last[0] = 0
    each_block(keys, score)
    add_windows(soft_1)
    pending.append(keys.finish)

    for half in range(2):
        loss = jnp.zeros((TILE, lists), jnp.float32)
        for q in range(block // TILE):
            tile = sums[q * TILE : (q + 1) * TILE, half * lists : (half + 1) * lists]
            loss = jnp.where(tables[half, 0] == q, tile, loss)
        losses[half] = jnp.transpose(loss * (1.0 / TILE))
    store_loss = pltpu.make_async_copy(losses, loss_ref, store_sem.at[1])
    store_loss.start()
    pending.append(store_loss.wait)
    for wait in pending:
        wait()


def hand_out(emb_in, loss_in, emb_ref, pos_ref, neg_ref):
    emb_ref[...] = emb_in[...]
    pos_ref[...] = loss_in[0]
    neg_ref[...] = loss_in[1]


def per_device(features, adjacency, tile_live, w_self, w_neigh, bias_vector, pos_pairs, neg_pairs):
    block, channels = features.shape
    sources = adjacency.shape[1]
    piece = block // N_REP
    lists = pos_pairs.shape[1]
    table = (pos_pairs.shape[2], 1, lists)
    place = pl.BlockSpec(memory_space=pl.ANY)
    vmem = pl.BlockSpec(memory_space=pltpu.VMEM)
    dma = pltpu.SemaphoreType.DMA
    spread_sems = [
        dma((3,)), dma((3,)), dma((3, 2, 3)), dma((2, N_Y, N_X)), dma((2, N_Y)), dma((2, N_Y)),
    ]
    bf16 = jnp.bfloat16
    f32 = jnp.float32
    limit = 60 * 1024 * 1024
    embedding, losses = pl.pallas_call(
        kernel,
        out_shape=(
            jax.ShapeDtypeStruct((piece, channels), bf16),
            jax.ShapeDtypeStruct((2, lists, TILE), f32),
        ),
        in_specs=[place] * 8,
        out_specs=(place,) * 2,
        scratch_shapes=[
            pltpu.VMEM((block, sources), bf16),
            pltpu.VMEM((channels, channels), bf16),
            pltpu.VMEM((channels, channels), bf16),
            pltpu.VMEM((1, channels), f32),
            pltpu.VMEM((2, *table), jnp.int32),
            pltpu.SMEM((1, 4), jnp.int32),
            pltpu.VMEM((4, piece, channels), bf16),
            pltpu.VMEM((sources, channels), bf16),
            pltpu.VMEM((block, channels), f32),
            pltpu.VMEM((block, channels), PART_TYPE),
            pltpu.VMEM((N_REP - 1, piece, channels), PART_TYPE),
            pltpu.VMEM((4, piece, channels), bf16),
            pltpu.VMEM((sources, channels), bf16),
            pltpu.VMEM((block, channels), bf16),
            pltpu.VMEM((block, channels), bf16),
            pltpu.VMEM((4, 2 * block, 2 * lists), bf16),
            pltpu.VMEM((block, 2 * block), bf16),
            pltpu.VMEM((block, 2 * block), bf16),
            pltpu.SMEM((1,), jnp.int32),
            pltpu.VMEM((block, 2 * lists), f32),
            pltpu.VMEM((2, lists, TILE), f32),
            dma((8,)), dma((2,)),
            *spread_sems,
            *spread_sems,
            dma((N_REP - 1,)), dma((N_REP - 1,)), dma((N_X,)), dma((N_X,)),
        ],
        compiler_params=pltpu.CompilerParams(
            collective_id=0, has_side_effects=True, vmem_limit_bytes=limit
        ),
    )(
        tile_live, features, adjacency, w_self, w_neigh, bias_vector.reshape(1, channels),
        pos_pairs.transpose(2, 0, 1), neg_pairs.transpose(2, 0, 1),
    )
    embedding, pos_loss, neg_loss = pl.pallas_call(
        hand_out,
        out_shape=(
            jax.ShapeDtypeStruct((piece, channels), bf16),
            jax.ShapeDtypeStruct((lists, TILE), f32),
            jax.ShapeDtypeStruct((lists, TILE), f32),
        ),
        in_specs=[vmem] * 2,
        out_specs=(vmem,) * 3,
        compiler_params=pltpu.CompilerParams(vmem_limit_bytes=limit),
    )(embedding, losses)
    return embedding, pos_loss[None], neg_loss[None]


def solution(mesh):
    return jax.shard_map(
        per_device,
        mesh=mesh,
        in_specs=(
            P("row", None),
            P("row", "rep"),
            P("row", "rep"),
            P(),
            P(),
            P(),
            P("row", "rep", None),
            P("row", "rep", None),
        ),
        out_specs=(P(("row", "rep"), None), P("row", "rep", None), P("row", "rep", None)),
        check_vma=False,
    )
```

```python
import functools

import jax
import jax.numpy as jnp
from jax import lax
from jax.experimental import pallas as pl
from jax.experimental.pallas import tpu as pltpu
from jax.sharding import PartitionSpec as P

MESH = pl.DeviceIdType.MESH
N_Z, N_X, N_C, N_Y = 8, 4, 2, 2
N_REP = N_X * N_Y
TILE = 128
PART_TYPE = jnp.bfloat16


def mod(a, n):
    return lax.rem(a, jnp.int32(n))


def div(a, n):
    return lax.div(a, jnp.int32(n))


class Place:
    def __init__(self, yh, z, c, yl, x):
        self.yh, self.z, self.c, self.yl, self.x = yh, z, c, yl, x

    def moved(self, **kw):
        at = dict(self.__dict__)
        at.update(kw)
        return Place(**at)

    @property
    def device(self):
        return {
            "row": self.yh * (N_Z * N_C) + self.z * N_C + self.c,
            "rep": self.yl * N_X + self.x,
        }


def remote(src, dst, send_sem, recv_sem, place):
    return pltpu.make_async_remote_copy(
        src_ref=src, dst_ref=dst, send_sem=send_sem, recv_sem=recv_sem,
        device_id=place.device, device_id_type=MESH,
    )


def arrived(ref, sem):
    pltpu.make_async_copy(ref, ref, sem).wait()


class Spread:
    SHIFTS = (0, 3, -3)
    STEPS = ((1, -1, 0), (1, -1, 0), (1, 0))

    def __init__(self, me, piece, held, full, sems):
        self.me, self.piece, self.held, self.full = me, piece, held, full
        self.s1, self.r1, self.s2, self.r2, self.s3, self.r3 = sems
        self.outer = me.yl == me.yh
        self.twin = me.moved(yh=1 - me.yh, yl=1 - me.yl)
        way = 1 - 2 * me.c
        self.planes = {dz: mod(me.z + N_Z + dz * way, N_Z) for dz in (0, 1, -1, 3, -3)}
        self.side = dict(
            yh=jnp.where(self.outer, self.twin.yh, me.yh), yl=jnp.where(self.outer, self.twin.yl, me.yl)
        )
        away = mod(me.z + N_Z - 2 * me.x, N_Z)
        first = [
            jnp.where(self.direct(a), 0, 1) for a in (away, mod(N_Z - away, N_Z))
        ]
        self.first = (
            jnp.where(me.c == 0, first[0], first[1]), jnp.where(me.c == 0, first[1], first[0])
        )

    def unit(self, zz, c, yl):
        rows = N_X * self.piece
        at = ((zz * N_C + c) * N_Y + yl) * rows
        return self.full.at[pl.ds(pl.multiple_of(at, TILE), rows), :]

    def slot(self, zz, yl, x):
        at = (((zz * N_C + self.me.c) * N_Y + yl) * N_X + x) * self.piece
        return self.full.at[pl.ds(pl.multiple_of(at, 16), self.piece), :]

    def beside(self, dz):
        return self.me.moved(z=self.planes[dz], **self.side)

    def to_holder(self, k):
        return remote(
            self.held.at[0], self.held.at[1 + k], self.s1.at[k], self.r1.at[k],
            self.beside(self.SHIFTS[k]),
        )

    def to_twin(self):
        return remote(self.held.at[0], self.held.at[1], self.s1.at[0], self.r1.at[0], self.twin)

    def copies(self, k, other):
        me = self.me
        if k:
            owner, at = self.beside(-self.SHIFTS[k]), 1 + k
        elif other:
            owner, at = self.beside(0), jnp.where(self.outer, 1, 0)
        else:
            owner, at = me, 0
        src = self.held.at[at]
        zz, x = mod(owner.z, 2), div(owner.z, 2)
        dst = self.slot(zz, owner.yl, me.x)
        recv = self.r2.at[zz, owner.yl, me.x]
        for i, dz in enumerate(self.STEPS[k]):
            to = me.moved(
                x=x, yl=owner.yh, yh=1 - owner.yh if other else owner.yh,
                z=self.planes[dz],
            )
            copy = remote(src, dst, self.s2.at[k, other, i], recv, to)
            if dz == 0 and not other and not k:
                stays = jnp.logical_and(me.x == x, self.outer)
                yield copy, pltpu.make_async_copy(src, dst, recv), stays
            else:
                yield copy, None, None

    def send(self, k, other):
        for copy, keep, stays in self.copies(k, other):
            if keep is None:
                copy.start()
            else:
                pl.when(stays)(keep.start)
                pl.when(jnp.logical_not(stays))(copy.start)

    def start_holders(self):
        self.to_holder(1).start()
        self.to_holder(2).start()
        pl.when(self.outer)(self.to_twin().start)

    def start(self):
        self.send(0, 0)
        pl.when(self.outer)(self.to_twin().wait_recv)
        self.send(0, 1)

    def relay(self):
        for k in (1, 2):
            self.to_holder(k).wait_recv()
            self.send(k, 1)
            self.send(k, 0)

    def away(self, source, c):
        dz = mod(self.me.z + N_Z - source, N_Z)
        return jnp.where(c == 0, dz, mod(N_Z - dz, N_Z))

    @staticmethod
    def direct(away):
        return jnp.logical_or(away <= 1, away == N_Z - 1)

    def order(self, i, sibling):
        first = self.first[sibling]
        return jnp.where(i == 0, first, 1 - first)

    def to_sibling(self, zz, yl):
        me = self.me
        rows = self.unit(zz, me.c, yl)
        return remote(rows, rows, self.s3.at[zz, yl], self.r3.at[zz, yl], me.moved(c=1 - me.c))

    def take_own(self, zz, yl):
        for x in range(N_X):
            arrived(self.slot(zz, yl, x), self.r2.at[zz, yl, x])
        self.to_sibling(zz, yl).start()

    def take_sibling(self, zz, yl):
        arrived(self.unit(zz, 1 - self.me.c, yl), self.r3.at[zz, yl])

    def finish(self):
        self.to_holder(1).wait_send()
        self.to_holder(2).wait_send()
        pl.when(self.outer)(self.to_twin().wait_send)
        for k in range(3):
            for other in range(2):
                for copy, keep, stays in self.copies(k, other):
                    if keep is None:
                        copy.wait_send()
                    else:
                        pl.when(jnp.logical_not(stays))(copy.wait_send)
        for zz in range(2):
            for yl in range(N_Y):
                self.to_sibling(zz, yl).wait_send()

    def greet(self, greet):
        me = self.me
        greet(self.beside(3))
        greet(self.beside(-3))
        pl.when(self.outer)(functools.partial(greet, self.twin))
        for zz in range(2):
            source = 2 * me.x + zz
            away = self.away(source, me.c)
            direct = self.direct(away)
            shift = jnp.where(direct, 0, jnp.where(away <= 4, 3, N_Z - 3))
            z = mod(source + jnp.where(me.c == 0, shift, N_Z - shift), N_Z)
            near = jnp.logical_and(direct, self.outer)
            swap = jnp.where(near, 0, 1)
            for x in range(N_X):
                outer = me.moved(x=x, z=z, yl=(me.yl + swap) % 2, yh=(me.yl + swap) % 2)
                itself = jnp.logical_and(jnp.logical_and(x == me.x, z == me.z), near)
                pl.when(jnp.logical_not(itself))(functools.partial(greet, outer))
                greet(me.moved(x=x, z=z, yl=1 - me.yl, yh=me.yl))
        stays = jnp.logical_and(me.x == div(me.z, 2), self.outer)
        return 18 + jnp.where(self.outer, 1, 0) - jnp.where(stays, 1, 0)


def each_block(spread, work):
    me = spread.me

    def take_own(i):
        zz = spread.order(i, 0)
        for yl in range(N_Y):
            spread.take_own(zz, yl)
        return zz, me.c

    def take_sibling(i):
        zz = spread.order(i, 1)
        for yl in range(N_Y):
            spread.take_sibling(zz, yl)
        return zz, 1 - me.c

    def step(q, carry):
        for n in range(2):
            work(*lax.cond(q == 0, take_own, take_sibling, n), n)
        return carry

    lax.fori_loop(0, 2, step, 0)


def kernel(
    live_ref, feat_ref, adj_ref, w_self_ref, w_neigh_ref, bias_ref, pos_ref, neg_ref,
    emb_ref, loss_ref,
    adj, w_self, w_neigh, bias, tables, live,
    held_f, full_f, acc, part, got, held_k, full_k, query, scaled_query, window, soft_0, soft_1, last, sums,
    losses, load_sem, store_sem, f1s, f1r, f2s, f2r, f3s, f3r, k1s, k1r, k2s, k2r, k3s, k3r, ps, pr, qs, qr,
):
    row, rep = lax.axis_index("row"), lax.axis_index("rep")
    me = Place(div(row, N_Z * N_C), mod(div(row, N_C), N_Z), mod(row, N_C), div(rep, N_X), mod(rep, N_X))
    peers = [
        me.moved(yl=1 - me.yl if dy else me.yl, x=mod(me.x + dx, N_X))
        for dy, dx in ((1, 2), (1, 1), (1, 3), (0, 2), (0, 1), (0, 3), (1, 0))
    ]
    block, channels = feat_ref.shape
    piece = block // N_REP
    lists = pos_ref.shape[2]
    own_rows = pl.ds(pl.multiple_of(rep * piece, 16), piece)
    loads = [
        pltpu.make_async_copy(src, dst, load_sem.at[i])
        for i, (src, dst) in enumerate((
            (feat_ref.at[own_rows, :], held_f.at[0]), (pos_ref, tables.at[0]), (neg_ref, tables.at[1]),
            (live_ref, live), (adj_ref, adj),
            (w_self_ref, w_self), (w_neigh_ref, w_neigh), (bias_ref, bias),
        ))
    ]
    loads[0].start()
    feats = Spread(me, piece, held_f, full_f, (f1s, f1r, f2s, f2r, f3s, f3r))
    keys = Spread(me, piece, held_k, full_k, (k1s, k1r, k2s, k2r, k3s, k3r))
    own = held_k.at[0]
    pending = []

    barrier = pltpu.get_barrier_semaphore()

    def greet(place):
        pl.semaphore_signal(barrier, inc=1, device_id=place.device, device_id_type=MESH)

    targets = feats.greet(greet)
    for peer in peers:
        greet(peer)
    greet(me.moved(c=1 - me.c))
    for load in loads[1:]:
        load.start()
    loads[0].wait()
    pl.semaphore_wait(barrier, targets + (N_REP - 1) + 1)

    feats.start_holders()
    feats.start()

    for load in loads[1:3]:
        load.wait()
    half_block = N_X * piece
    row_at = lax.broadcasted_iota(jnp.int32, (TILE, lists), 0)
    nothing = jnp.zeros((block, lists), jnp.bfloat16)
    first = [tables[half, 1] * block + tables[half, 2] for half in range(2)]

    def fill(k, carry):
        window[k, :block, lists:] = nothing
        window[k, block:, :lists] = nothing
        for half in range(2):
            for j in range(0, block, TILE):
                since = row_at + (k * block + j) - first[half]
                inside = jnp.logical_and(since >= 0, since < TILE)
                at = half * block + j
                window[k, at : at + TILE, half * lists : (half + 1) * lists] = jnp.where(
                    inside, 1.0, 0.0
                ).astype(jnp.bfloat16)
        return carry

    lax.fori_loop(0, 4, fill, 0)
    acc[...] = jnp.zeros_like(acc)
    sums[...] = jnp.zeros_like(sums)

    feats.relay()
    for load in loads[3:]:
        load.wait()

    def aggregate(zz, c, n):
        k = zz * N_C + c
        flag = (live[0, k] > 0).astype(jnp.float32).astype(jnp.bfloat16)
        at = pl.ds(pl.multiple_of(k * block, TILE), block)
        acc[...] += jnp.dot(
            adj[:, at], full_f[at, :] * flag, preferred_element_type=jnp.float32
        )

    each_block(feats, aggregate)
    pending.append(feats.finish)


    def partial_to(d):
        at = (peers[d].yl * N_X + peers[d].x) * piece
        return remote(
            part.at[pl.ds(pl.multiple_of(at, 16), piece), :],
            got.at[d], ps.at[d], pr.at[d], peers[d],
        )

    for d in range(N_REP - 1):
        rows = pl.ds(pl.multiple_of((peers[d].yl * N_X + peers[d].x) * piece, 16), piece)
        part[rows, :] = acc[rows, :].astype(part.dtype)
        partial_to(d).start()
    pending.extend(partial_to(d).wait_send for d in range(N_REP - 1))
    projected = jnp.dot(held_f[0], w_self[...], preferred_element_type=jnp.float32)
    neighbour = acc[own_rows, :]
    for d in range(N_REP - 1):
        partial_to(d).wait_recv()
        neighbour = neighbour + got[d].astype(jnp.float32)
    projected = projected + jnp.dot(
        neighbour.astype(jnp.bfloat16), w_neigh[...], preferred_element_type=jnp.float32
    )
    projected = projected + bias[...]
    scaled = projected * lax.rsqrt(jnp.mean(projected * projected, axis=-1, keepdims=True) + 1e-06)
    held_k[0] = scaled.astype(jnp.bfloat16)

    def query_to(d):
        x = mod(me.x + d, N_X)
        return remote(own, query.at[own_rows, :], qs.at[d - 1], qr.at[d - 1], me.moved(x=x))

    def query_half(yl):
        rows = query.at[pl.ds(pl.multiple_of(yl * half_block, TILE), half_block), :]
        return remote(rows, rows, qs.at[N_X - 1], qr.at[N_X - 1], me.moved(yl=1 - me.yl))

    keys.start_holders()
    for d in range(1, N_X):
        query_to(d).start()
    keys.start()
    query[own_rows, :] = held_k[0]
    store_emb = pltpu.make_async_copy(own, emb_ref, store_sem.at[0])
    store_emb.start()
    for wait in pending:
        wait()
    pending.clear()
    pending.append(store_emb.wait)
    for d in range(1, N_X):
        query_to(d).wait_recv()
    query_half(me.yl).start()
    pending.extend(query_to(d).wait_send for d in range(1, N_X))
    pending.append(query_half(me.yl).wait_send)

    keys.relay()
    query_half(1 - me.yl).wait_recv()
    scaled_query[...] = query[...] * channels ** -0.5
    soft = (soft_0, soft_1)

    def add_windows(ref):
        sums[...] += jnp.dot(ref[...], window[last[0]], preferred_element_type=jnp.float32)

    def score(zz, c, n):
        k = zz * N_C + c
        add_windows(soft[1 - n])
        for j in range(0, block, TILE):
            at = pl.ds(pl.multiple_of(k * block + j, TILE), TILE)
            t = lax.dot_general(
                scaled_query[...], full_k[at, :], (((1,), (1,)), ((), ())),
                preferred_element_type=jnp.float32,
            )
            low, high = jnp.minimum(t, 0.0), jnp.maximum(t, 0.0)
            e = jnp.exp(low - high)
            tail = jnp.where(e < 2.0 ** -12, e, jnp.log(1.0 + e))
            soft[n][:, j : j + TILE] = (tail - low).astype(jnp.bfloat16)
            soft[n][:, block + j : block + j + TILE] = (tail + high).astype(jnp.bfloat16)
        last[0] = k

    soft_1[...] = jnp.zeros_like(soft_1)
    last[0] = 0
    each_block(keys, score)
    add_windows(soft_1)
    pending.append(keys.finish)

    for half in range(2):
        loss = jnp.zeros((TILE, lists), jnp.float32)
        for q in range(block // TILE):
            tile = sums[q * TILE : (q + 1) * TILE, half * lists : (half + 1) * lists]
            loss = jnp.where(tables[half, 0] == q, tile, loss)
        losses[half] = jnp.transpose(loss * (1.0 / TILE))
    store_loss = pltpu.make_async_copy(losses, loss_ref, store_sem.at[1])
    store_loss.start()
    pending.append(store_loss.wait)
    for wait in pending:
        wait()


def hand_out(emb_in, loss_in, emb_ref, pos_ref, neg_ref):
    emb_ref[...] = emb_in[...]
    pos_ref[...] = loss_in[0]
    neg_ref[...] = loss_in[1]


def per_device(features, adjacency, tile_live, w_self, w_neigh, bias_vector, pos_pairs, neg_pairs):
    block, channels = features.shape
    sources = adjacency.shape[1]
    piece = block // N_REP
    lists = pos_pairs.shape[1]
    table = (pos_pairs.shape[2], 1, lists)
    place = pl.BlockSpec(memory_space=pl.ANY)
    vmem = pl.BlockSpec(memory_space=pltpu.VMEM)
    dma = pltpu.SemaphoreType.DMA
    spread_sems = [
        dma((3,)), dma((3,)), dma((3, 2, 3)), dma((2, N_Y, N_X)), dma((2, N_Y)), dma((2, N_Y)),
    ]
    bf16 = jnp.bfloat16
    f32 = jnp.float32
    limit = 60 * 1024 * 1024
    embedding, losses = pl.pallas_call(
        kernel,
        out_shape=(
            jax.ShapeDtypeStruct((piece, channels), bf16),
            jax.ShapeDtypeStruct((2, lists, TILE), f32),
        ),
        in_specs=[place] * 8,
        out_specs=(place,) * 2,
        scratch_shapes=[
            pltpu.VMEM((block, sources), bf16),
            pltpu.VMEM((channels, channels), bf16),
            pltpu.VMEM((channels, channels), bf16),
            pltpu.VMEM((1, channels), f32),
            pltpu.VMEM((2, *table), jnp.int32),
            pltpu.SMEM((1, 4), jnp.int32),
            pltpu.VMEM((4, piece, channels), bf16),
            pltpu.VMEM((sources, channels), bf16),
            pltpu.VMEM((block, channels), f32),
            pltpu.VMEM((block, channels), PART_TYPE),
            pltpu.VMEM((N_REP - 1, piece, channels), PART_TYPE),
            pltpu.VMEM((4, piece, channels), bf16),
            pltpu.VMEM((sources, channels), bf16),
            pltpu.VMEM((block, channels), bf16),
            pltpu.VMEM((block, channels), bf16),
            pltpu.VMEM((4, 2 * block, 2 * lists), bf16),
            pltpu.VMEM((block, 2 * block), bf16),
            pltpu.VMEM((block, 2 * block), bf16),
            pltpu.SMEM((1,), jnp.int32),
            pltpu.VMEM((block, 2 * lists), f32),
            pltpu.VMEM((2, lists, TILE), f32),
            dma((8,)), dma((2,)),
            *spread_sems,
            *spread_sems,
            dma((N_REP - 1,)), dma((N_REP - 1,)), dma((N_X,)), dma((N_X,)),
        ],
        compiler_params=pltpu.CompilerParams(
            collective_id=0, has_side_effects=True, vmem_limit_bytes=limit
        ),
    )(
        tile_live, features, adjacency, w_self, w_neigh, bias_vector.reshape(1, channels),
        pos_pairs.transpose(2, 0, 1), neg_pairs.transpose(2, 0, 1),
    )
    embedding, pos_loss, neg_loss = pl.pallas_call(
        hand_out,
        out_shape=(
            jax.ShapeDtypeStruct((piece, channels), bf16),
            jax.ShapeDtypeStruct((lists, TILE), f32),
            jax.ShapeDtypeStruct((lists, TILE), f32),
        ),
        in_specs=[vmem] * 2,
        out_specs=(vmem,) * 3,
        compiler_params=pltpu.CompilerParams(vmem_limit_bytes=limit),
    )(embedding, losses)
    return embedding, pos_loss[None], neg_loss[None]


def solution(mesh):
    return jax.shard_map(
        per_device,
        mesh=mesh,
        in_specs=(
            P("row", None),
            P("row", "rep"),
            P("row", "rep"),
            P(),
            P(),
            P(),
            P("row", "rep", None),
            P("row", "rep", None),
        ),
        out_specs=(P(("row", "rep"), None), P("row", "rep", None), P("row", "rep", None)),
        check_vma=False,
    )
```
